32 devices in a mesh: fsdp: 4 (over z), context: 2 (over x), tensor: 4 (over y, core).
Axes of the slice: x: 2, y: 2, z: 4, core: 2. Of those that a mesh axis runs over, the one named last changes fastest.
Arguments:
- hidden_in: bfloat16 [6144, 1024], P(('fsdp', 'context')), may hold values from -6 to 6
- out_grad: bfloat16 [6144, 1024], P(('fsdp', 'context')), may hold values from -6 to 6
- doc_lengths: int32 [4, 4], P('fsdp'), may hold values from 1 to 1152, as said below
- attn_gain: float32 [1024], replicated, may hold values from 0.5 to 1.5
- q_gain: float32 [128], replicated, may hold values from 0.6 to 1.6
- k_gain: float32 [128], replicated, may hold values from 0.6 to 1.6
- w_query: bfloat16 [1024, 2048], P('fsdp', 'tensor'), may hold values from -0.1875 to 0.1875
- key_projection: bfloat16 [1024, 1024], P('fsdp', 'tensor'), may hold values from -0.1875 to 0.1875
- value_projection: bfloat16 [1024, 1024], P('fsdp', 'tensor'), may hold values from -0.1875 to 0.1875
- w_out: bfloat16 [2048, 1024], P('tensor', 'fsdp'), may hold values from -0.75 to 0.75
- ffn_gain: float32 [1024], replicated, may hold values from 0.5 to 1.5
- w_gate: bfloat16 [1024, 3072], P('fsdp', 'tensor'), may hold values from -0.1875 to 0.1875
- w_up: bfloat16 [1024, 3072], P('fsdp', 'tensor'), may hold values from -0.1875 to 0.1875
- w_down: bfloat16 [3072, 1024], P('tensor', 'fsdp'), may hold values from -0.109375 to 0.109375
Outputs:
- block_out: bfloat16 [6144, 1024], P(('fsdp', 'context'))
- input_grad: float32 [6144, 1024], P(('fsdp', 'context'))
- attn_gain_grad: float32 [1024], replicated
- q_gain_grad: float32 [128], replicated
- k_gain_grad: float32 [128], replicated
- w_query_grad: float32 [1024, 2048], P('fsdp', 'tensor')
- w_key_grad: float32 [1024, 1024], P('fsdp', 'tensor')
- w_value_grad: float32 [1024, 1024], P('fsdp', 'tensor')
- w_out_grad: float32 [2048, 1024], P('tensor', 'fsdp')
- ffn_gain_grad: float32 [1024], replicated
- w_gate_grad: float32 [1024, 3072], P('fsdp', 'tensor')
- w_up_grad: float32 [1024, 3072], P('fsdp', 'tensor')
- w_down_grad: float32 [3072, 1024], P('tensor', 'fsdp')
The draws below stay inside these ranges and needn't reach their ends.
Inputs may be any that keep to these rules, and one draw needn't show every extreme that they name: `doc_lengths`: each row holds the lengths of 4 documents packed in order into that batch's 1536 places, summing to 1536; one of them, at a position drawn from the seed, has exactly 1152 places, so it starts among the batch's first 768 places and ends among its last 768; the others together take 768 / 2 places.
All inputs are finite; a program needn't handle non-finite values.
Results may differ from the reference program's by a relative error of at most 0.033.
Values may be sent and summed in bfloat16 or wider, within the bound.
A program may use at most 128 MiB of HBM per device.

```python
import math
import jax
import jax.numpy as jnp
from jax import lax

MODEL_WIDTH = 1024
QUERY_HEADS = 16
KEY_VALUE_HEADS = 8
HEAD_SIZE = 128
FF = 3072
TOK_DEV = 768
NDOC = 4
TOKENS_PER_SHARD = 1536
TOKEN_TOTAL = 6144
N_FSDP = 4


def draw_doc_lengths(key, part):
    key = jax.random.fold_in(key, 11)
    batch_keys = jax.random.split(key, N_FSDP)
    short_total = TOK_DEV // 2
    short_limit = max(TOK_DEV // (2 * (NDOC - 1)), 1)

    def one_batch(batch_key):
        short_key, place_key = jax.random.split(batch_key)
        free_lengths = jax.random.randint(short_key, (NDOC - 2,), 1, short_limit + 1).astype(jnp.int32)
        last_short = (short_total - jnp.sum(free_lengths)).astype(jnp.int32)
        short_lengths = jnp.concatenate([free_lengths, last_short[None]]).astype(jnp.int32)
        long_place = jax.random.randint(place_key, (), 0, NDOC)
        long_length = TOKENS_PER_SHARD - short_total
        numbers = jnp.arange(NDOC)
        picked = jnp.clip(numbers - (numbers > long_place).astype(jnp.int32), 0, NDOC - 2)
        return jnp.where(numbers == long_place, long_length, short_lengths[picked]).astype(jnp.int32)
    return jax.vmap(one_batch)(batch_keys)


def steps_of(own_key, shape, shards, least, high):
    gain, own = 1.0, jax.random.fold_in(own_key, 6)
    for dim, blocks in shards:
        steps = jnp.exp(jax.random.uniform(jax.random.fold_in(own, dim), (blocks,), jnp.float32, least / len(shards), high / len(shards)))
        gain = gain * jnp.repeat(steps, shape[dim] // blocks).reshape([-1 if axis == dim else 1 for axis in range(len(shape))])
    return gain


def centred(key, extent, spread, reach, pieces=(), held_as=jnp.bfloat16):
    values = jax.random.normal(key, extent, jnp.float32) * spread
    if len(pieces) > 0:
        values = steps_of(key, extent, pieces, -0.22, 0.18) * values
    return jnp.clip(values, min=-reach, max=reach).astype(held_as)


def setup_inputs(seed: int = 0) -> dict:
    streams_of = jax.random.split(jax.random.key(seed), 15)
    hidden_in = centred(streams_of[0], (TOKEN_TOTAL, MODEL_WIDTH), 1.0, 6.0, ((0, 8),))
    out_grad = centred(streams_of[1], (TOKEN_TOTAL, MODEL_WIDTH), 1.0, 6.0, ((0, 8),))
    doc_lengths = draw_doc_lengths(jax.random.fold_in(streams_of[14], 71), 0)
    attn_gain = jnp.clip(jax.random.uniform(streams_of[3], (MODEL_WIDTH,), jnp.float32, 0.5, 1.5), 0.5, 1.5)
    q_gain = jnp.clip(jax.random.uniform(streams_of[4], (HEAD_SIZE,), jnp.float32, 0.6, 1.6), 0.6, 1.6)
    k_gain = jnp.clip(jax.random.uniform(streams_of[5], (HEAD_SIZE,), jnp.float32, 0.6, 1.6), 0.6, 1.6)
    w_query = centred(streams_of[6], (MODEL_WIDTH, QUERY_HEADS * HEAD_SIZE), MODEL_WIDTH ** -0.5, 0.1875, ((0, 4), (1, 4)))
    key_projection = centred(streams_of[7], (MODEL_WIDTH, KEY_VALUE_HEADS * HEAD_SIZE), MODEL_WIDTH ** -0.5, 0.1875, ((0, 4), (1, 4)))
    value_projection = centred(streams_of[8], (MODEL_WIDTH, KEY_VALUE_HEADS * HEAD_SIZE), MODEL_WIDTH ** -0.5, 0.1875, ((0, 4), (1, 4)))
    w_out = centred(streams_of[9], (QUERY_HEADS * HEAD_SIZE, MODEL_WIDTH), (QUERY_HEADS * HEAD_SIZE // 32) ** -0.5, 0.75, ((0, 4), (1, 4)))
    ffn_gain = jnp.clip(jax.random.uniform(streams_of[10], (MODEL_WIDTH,), jnp.float32, 0.5, 1.5), 0.5, 1.5)
    w_gate = centred(streams_of[11], (MODEL_WIDTH, FF), MODEL_WIDTH ** -0.5, 0.1875, ((0, 4), (1, 4)))
    w_up = centred(streams_of[12], (MODEL_WIDTH, FF), MODEL_WIDTH ** -0.5, 0.1875, ((0, 4), (1, 4)))
    w_down = centred(streams_of[13], (FF, MODEL_WIDTH), FF ** -0.5, 0.109375, ((0, 4), (1, 4)))
    return dict(hidden_in=hidden_in, out_grad=out_grad, doc_lengths=doc_lengths, attn_gain=attn_gain, q_gain=q_gain, k_gain=k_gain, w_query=w_query, key_projection=key_projection, value_projection=value_projection, w_out=w_out, ffn_gain=ffn_gain, w_gate=w_gate, w_up=w_up, w_down=w_down)


epsilon = 1e-06
rope_base = 1000000.0

@jax.custom_vjp
def reduced_output(v):
    return lax.optimization_barrier(v.astype(jnp.bfloat16)).astype(jnp.float32)

@jax.custom_vjp
def reduced_gradient(v):
    return v

def low_keep(v):
    return (reduced_output(v), None)

def low_pass(kept, grad):
    return (grad,)

def back_keep(v):
    return (v, None)

def back_low(kept, grad):
    return (reduced_output(grad),)
reduced_output.defvjp(low_keep, low_pass)
reduced_gradient.defvjp(back_keep, back_low)

def doc_layout(lengths_row, positions):
    doc_ends = jnp.cumsum(lengths_row).astype(jnp.int32)
    doc_starts = (doc_ends - lengths_row).astype(jnp.int32)
    after_end = positions[:, None] >= doc_ends[None, :]
    inside = (positions[:, None] >= doc_starts[None, :]) & jnp.logical_not(after_end)
    packed_documents = lax.optimization_barrier(jnp.sum(after_end.astype(jnp.int32), axis=1)).astype(jnp.int32)
    doc_begin = lax.optimization_barrier(jnp.sum(jnp.where(inside, doc_starts[None, :], 0), axis=1)).astype(jnp.int32)
    return (packed_documents, (positions - doc_begin).astype(jnp.int32))

def rope_tables(positions, head_dim):
    half_dim = head_dim // 2
    freqs = rope_base ** (-(jnp.arange(half_dim, dtype=jnp.float32) * (2.0 / head_dim)))
    angles = positions.astype(jnp.float32)[:, None] * freqs[None, :]
    return (jnp.cos(angles)[:, None, :], jnp.sin(angles)[:, None, :])

def rotate(values, cosine, sine):
    half_dim = values.shape[-1] // 2
    lower, upper = (values[..., :half_dim], values[..., half_dim:])
    return jnp.concatenate([lower * cosine - upper * sine, upper * cosine + lower * sine], axis=-1)

def inverse_rms(values):
    return lax.rsqrt(lax.optimization_barrier(jnp.mean(values * values, axis=-1, keepdims=True)) + epsilon)

def matrix_product(left, right):
    return jnp.dot(left, right, precision=lax.Precision.HIGHEST)

def attend_head_group(operands):
    query_rows, gathered_keys, gathered_values, packed_documents = operands
    token_positions = jnp.arange(TOKENS_PER_SHARD, dtype=jnp.int32)
    rows_per_block = math.gcd(TOKENS_PER_SHARD, 512)
    count_of_blocks = TOKENS_PER_SHARD // rows_per_block
    inv_sqrt = 1.0 / math.sqrt(HEAD_SIZE)

    def single_block(parts):
        query_blk, doc_blk, place_blk = parts
        scores = jnp.einsum('qkgd,skd->kgqs', query_blk, gathered_keys, precision=lax.Precision.HIGHEST) * inv_sqrt
        scores = reduced_gradient(scores)
        allowed = (token_positions[None, :] <= place_blk[:, None]) & (packed_documents[None, :] == doc_blk[:, None])
        scores = jnp.where(allowed, scores, -1e+30)
        highest = lax.optimization_barrier(jnp.max(scores, axis=-1, keepdims=True))
        weights = jnp.where(allowed, jnp.exp(scores - highest), 0.0)
        probs = reduced_output(weights / lax.optimization_barrier(jnp.sum(weights, axis=-1, keepdims=True)))
        return jnp.einsum('kgqs,skd->qkgd', probs, gathered_values, precision=lax.Precision.HIGHEST)
    layer_outputs = lax.map(jax.checkpoint(single_block), (query_rows.reshape(count_of_blocks, rows_per_block, KEY_VALUE_HEADS, QUERY_HEADS // KEY_VALUE_HEADS, HEAD_SIZE), packed_documents.reshape(count_of_blocks, rows_per_block), token_positions.reshape(count_of_blocks, rows_per_block)))
    return layer_outputs.reshape(TOKENS_PER_SHARD, QUERY_HEADS, HEAD_SIZE)

def reference(hidden_in, out_grad, doc_lengths, attn_gain, q_gain, k_gain, w_query, key_projection, value_projection, w_out, ffn_gain, w_gate, w_up, w_down):
    packed_documents, offsets = jax.vmap(doc_layout, in_axes=(0, None))(doc_lengths, jnp.arange(TOKENS_PER_SHARD, dtype=jnp.int32))
    cosine, sine = rope_tables(offsets.reshape(TOKEN_TOTAL), HEAD_SIZE)

    def forward(residual_in, attn_gain, q_gain, k_gain, w_query, key_projection, value_projection, w_out, ffn_gain, w_gate, w_up, w_down):
        scale_one = inverse_rms(residual_in)
        first_normed = reduced_output(residual_in * scale_one * attn_gain)
        query_raw = reduced_gradient(matrix_product(first_normed, w_query)).reshape(TOKEN_TOTAL, QUERY_HEADS, HEAD_SIZE)
        unnormed_key = reduced_gradient(matrix_product(first_normed, key_projection)).reshape(TOKEN_TOTAL, KEY_VALUE_HEADS, HEAD_SIZE)
        gathered_values = reduced_output(reduced_gradient(matrix_product(first_normed, value_projection))).reshape(TOKEN_TOTAL, KEY_VALUE_HEADS, HEAD_SIZE)
        query_rows = reduced_output(rotate(query_raw * inverse_rms(query_raw) * q_gain, cosine, sine))
        gathered_keys = reduced_output(rotate(unnormed_key * inverse_rms(unnormed_key) * k_gain, cosine, sine))
        attention_result = lax.map(attend_head_group, (query_rows.reshape(N_FSDP, TOKENS_PER_SHARD, KEY_VALUE_HEADS, QUERY_HEADS // KEY_VALUE_HEADS, HEAD_SIZE), gathered_keys.reshape(N_FSDP, TOKENS_PER_SHARD, KEY_VALUE_HEADS, HEAD_SIZE), gathered_values.reshape(N_FSDP, TOKENS_PER_SHARD, KEY_VALUE_HEADS, HEAD_SIZE), packed_documents))
        attention_result = reduced_output(reduced_gradient(attention_result.reshape(TOKEN_TOTAL, QUERY_HEADS * HEAD_SIZE)))
        mixed = residual_in + reduced_gradient(matrix_product(attention_result, w_out))
        scale_two = inverse_rms(mixed)
        normed_two = reduced_output(mixed * scale_two * ffn_gain)
        gate = reduced_gradient(matrix_product(normed_two, w_gate))
        up_part = reduced_gradient(matrix_product(normed_two, w_up))
        activated = reduced_output(jax.nn.silu(gate) * up_part)
        return mixed + reduced_gradient(matrix_product(activated, w_down))
    block_out, pullback = jax.vjp(forward, hidden_in.astype(jnp.float32), attn_gain, q_gain, k_gain, w_query.astype(jnp.float32), key_projection.astype(jnp.float32), value_projection.astype(jnp.float32), w_out.astype(jnp.float32), ffn_gain, w_gate.astype(jnp.float32), w_up.astype(jnp.float32), w_down.astype(jnp.float32))
    grads = pullback(out_grad.astype(jnp.float32))
    return (block_out.astype(jnp.bfloat16), grads[0], grads[1], grads[2], grads[3], grads[4], grads[5], grads[6], grads[7], grads[8], grads[9], grads[10], grads[11])
```

```python
import math

import jax
import jax.numpy as jnp
from jax import lax
from jax.sharding import PartitionSpec as P

epsilon = 1e-06
rope_base = 1000000.0
masked_score = -1e30


def inverse_rms(values):
    return lax.rsqrt(jnp.mean(values * values, axis=-1, keepdims=True) + epsilon)


def norm_backward(values, scaling, gain, grads):
    scaled = gain * grads
    cubed = scaling * scaling * scaling
    return scaling * scaled - values * cubed * jnp.mean(scaled * values, axis=-1, keepdims=True)


def doc_layout(lengths_row, positions):
    doc_ends = jnp.cumsum(lengths_row)
    doc_starts = doc_ends - lengths_row
    after_end = positions[:, None] >= doc_ends[None, :]
    inside = (positions[:, None] >= doc_starts[None, :]) & jnp.logical_not(after_end)
    packed_documents = jnp.sum(after_end.astype(jnp.int32), axis=1)
    doc_begin = jnp.sum(jnp.where(inside, doc_starts[None, :], 0), axis=1)
    return (packed_documents, positions - doc_begin)


def rope_tables(positions, head_dim):
    half_dim = head_dim // 2
    freqs = rope_base ** (-(jnp.arange(half_dim, dtype=jnp.float32) * (2.0 / head_dim)))
    angles = positions.astype(jnp.float32)[:, None] * freqs[None, :]
    return (jnp.cos(angles)[:, None, :], jnp.sin(angles)[:, None, :])


def rotate(values, cosine, sine):
    half_dim = values.shape[-1] // 2
    lower, upper = (values[..., :half_dim], values[..., half_dim:])
    return jnp.concatenate([lower * cosine - upper * sine, upper * cosine + lower * sine], axis=-1)


def rotate_back(grads, cosine, sine):
    half_dim = grads.shape[-1] // 2
    lower, upper = (grads[..., :half_dim], grads[..., half_dim:])
    return jnp.concatenate([lower * cosine + upper * sine, upper * cosine - lower * sine], axis=-1)


def flip(values, axis_name, bit):
    size = lax.axis_size(axis_name)
    return lax.ppermute(values, axis_name, [(i, i ^ bit) for i in range(size)])


def is_power(size):
    return size & (size - 1) == 0


def has_pairs():
    return lax.axis_size("context") == 2 and is_power(lax.axis_size("fsdp"))


def order_matrix(width):
    size = lax.axis_size("fsdp")
    me, side = lax.axis_index("fsdp"), lax.axis_index("context")
    piece = width // (2 * size)
    column = jnp.arange(width, dtype=jnp.int32)
    chunk = column // piece
    source = ((me ^ (chunk % size)) * 2 + (side ^ (chunk // size))) * piece + column % piece
    return column[:, None] == source[None, :]


def permute(values, spec):
    if not has_pairs():
        return values
    order = order_matrix(values.shape[-1])
    if values.ndim == 1:
        return jnp.einsum(
            spec, values[None], order.astype(jnp.float32), precision=lax.Precision.HIGHEST
        )[0]
    order = order.astype(jnp.bfloat16)
    high = values.astype(jnp.bfloat16)
    out = jnp.einsum(spec, high, order, preferred_element_type=jnp.float32)
    if values.dtype == jnp.float32:
        low = (values - high.astype(jnp.float32)).astype(jnp.bfloat16)
        out = out + jnp.einsum(spec, low, order, preferred_element_type=jnp.float32)
    return out.astype(values.dtype)


def arrange(values):
    return permute(values, "tr,rc->tc")


def restore(values):
    return permute(values, "tc,rc->tr")


def gather_weight(shard, dim):
    if not has_pairs():
        return lax.all_gather(shard, "fsdp", axis=dim, tiled=True)
    size, side = lax.axis_size("fsdp"), lax.axis_index("context")
    half = shard.shape[dim] // 2
    mine = lax.dynamic_slice_in_dim(shard, side * half, half, dim)
    rest = lax.dynamic_slice_in_dim(shard, (1 - side) * half, half, dim)
    fetched = [flip(mine, "fsdp", bit) for bit in range(1, size)]
    swapped = [flip(piece, "context", 1) for piece in fetched]
    return jnp.concatenate([mine, *fetched, rest, *swapped], axis=dim)


def scatter_grad(grad, dim):
    low = grad.astype(jnp.bfloat16)
    size = lax.axis_size("fsdp")
    if not has_pairs():
        part = lax.psum_scatter(low, "fsdp", scatter_dimension=dim, tiled=True)
        return lax.psum(part, "context").astype(jnp.float32)
    side = lax.axis_index("context")
    half = low.shape[dim] // 2
    piece = half // size
    kept = lax.slice_in_dim(low, 0, half, axis=dim)
    other = flip(lax.slice_in_dim(low, half, 2 * half, axis=dim), "context", 1)
    summed = [
        lax.slice_in_dim(kept, b * piece, (b + 1) * piece, axis=dim).astype(jnp.float32)
        + lax.slice_in_dim(other, b * piece, (b + 1) * piece, axis=dim).astype(jnp.float32)
        for b in range(size)
    ]
    arrived = [flip(summed[b].astype(jnp.bfloat16), "fsdp", b) for b in range(1, size)]
    total = summed[0]
    for part in arrived:
        total = total + part.astype(jnp.float32)
    total = total.astype(jnp.bfloat16)
    other = flip(total, "context", 1)
    first = jnp.where(side == 0, total, other)
    second = jnp.where(side == 0, other, total)
    return jnp.concatenate([first, second], axis=dim).astype(jnp.float32)


def tensor_sum(values, chunks=2):
    low = values.astype(jnp.bfloat16)
    if lax.axis_size("tensor") != 4:
        return lax.psum(low, "tensor").astype(jnp.float32)
    core = lax.axis_index("tensor") % 2
    rows, width = low.shape
    half = rows // (2 * chunks)
    pieces = low.reshape(chunks, 2, half, width)
    done = []
    for chunk in range(chunks):
        kept = lax.dynamic_index_in_dim(pieces[chunk], core, 0, keepdims=False)
        sent = lax.dynamic_index_in_dim(pieces[chunk], 1 - core, 0, keepdims=False)
        other = flip(sent, "tensor", 1)
        pair = (kept.astype(jnp.float32) + other.astype(jnp.float32)).astype(jnp.bfloat16)
        far = flip(pair, "tensor", 2)
        total = (pair.astype(jnp.float32) + far.astype(jnp.float32)).astype(jnp.bfloat16)
        other = flip(total, "tensor", 1)
        done.append(jnp.where(core == 0, total, other))
        done.append(jnp.where(core == 0, other, total))
    return jnp.concatenate(done, axis=0).astype(jnp.float32)


def sum_everywhere(values):
    for name in ("tensor", "fsdp", "context"):
        size = lax.axis_size(name)
        if is_power(size):
            bit = 1
            while bit < size:
                values = values + flip(values, name, bit)
                bit *= 2
        else:
            values = lax.psum(values, name)
    return values


def on_device(
    hidden_in,
    out_grad,
    doc_lengths,
    attn_gain,
    q_gain,
    k_gain,
    w_query,
    key_projection,
    value_projection,
    w_out,
    ffn_gain,
    w_gate,
    w_up,
    w_down,
):
    hidden_in, out_grad = arrange(hidden_in), arrange(out_grad)
    attn_gain, ffn_gain = arrange(attn_gain), arrange(ffn_gain)
    tok_rows = hidden_in.shape[0]
    head_dim = q_gain.shape[0]
    q_cols, k_cols = w_query.shape[1], key_projection.shape[1]
    qkv_full = gather_weight(
        jnp.concatenate([w_query, key_projection, value_projection], axis=1), 0
    )
    qkv_full, w_out, w_gate, w_up, w_down = lax.optimization_barrier(
        (qkv_full, w_out, w_gate, w_up, w_down)
    )
    o_full = gather_weight(w_out, 1)
    gu_full = gather_weight(jnp.concatenate([w_gate, w_up], axis=1), 0)
    d_full = gather_weight(w_down, 1)
    q_heads = q_cols // head_dim
    kv_heads = k_cols // head_dim
    group_size = q_heads // kv_heads
    inv_sqrt = 1.0 / math.sqrt(head_dim)
    first_row = lax.axis_index("context") * tok_rows
    positions = first_row + jnp.arange(tok_rows, dtype=jnp.int32)
    lengths_row = doc_lengths[0]
    query_docs, query_offsets = doc_layout(lengths_row, positions)
    cosine, sine = rope_tables(query_offsets, head_dim)
    last_query = first_row + tok_rows - 1
    residual_in = hidden_in.astype(jnp.float32)
    scale_one = inverse_rms(residual_in)
    first_normed = (residual_in * scale_one * attn_gain).astype(jnp.bfloat16)
    projected = jnp.dot(first_normed, qkv_full, preferred_element_type=jnp.float32)
    query_raw = projected[:, :q_cols].reshape(tok_rows, q_heads, head_dim)
    unnormed_key = projected[:, q_cols : q_cols + k_cols].reshape(tok_rows, kv_heads, head_dim)
    values_local = (
        projected[:, q_cols + k_cols :].astype(jnp.bfloat16).reshape(tok_rows, kv_heads, head_dim)
    )
    query_scale = inverse_rms(query_raw)
    key_scale = inverse_rms(unnormed_key)
    query_rows = rotate(query_raw * query_scale * q_gain, cosine, sine).astype(jnp.bfloat16)
    keys_local = rotate(unnormed_key * key_scale * k_gain, cosine, sine).astype(jnp.bfloat16)
    grouped_q = query_rows.reshape(tok_rows, kv_heads, group_size, head_dim)

    def block_mask(key_first, key_count):
        key_places = key_first + jnp.arange(key_count, dtype=jnp.int32)
        key_docs, key_offsets = doc_layout(lengths_row, key_places)
        return (key_places[None, :] <= positions[:, None]) & (
            key_docs[None, :] == query_docs[:, None]
        )

    def attend(running, key_blk, val_blk, key_first):
        best, total, summed = running
        allowed = block_mask(key_first, key_blk.shape[0])
        scores = (
            jnp.einsum("qkgd,skd->kgqs", grouped_q, key_blk, preferred_element_type=jnp.float32)
            * inv_sqrt
        )
        scores = jnp.where(allowed, scores, masked_score)
        new_best = jnp.maximum(best, jnp.max(scores, axis=-1))
        weights = jnp.where(allowed, jnp.exp(scores - new_best[..., None]), 0.0)
        factor = jnp.exp(best - new_best)
        total = total * factor + jnp.sum(weights, axis=-1)
        summed = summed * factor[..., None] + jnp.einsum(
            "kgqs,skd->kgqd",
            weights.astype(jnp.bfloat16),
            val_blk,
            preferred_element_type=jnp.float32,
        )
        return (new_best, total, summed)

    start_state = (
        jnp.full((kv_heads, group_size, tok_rows), masked_score, jnp.float32),
        jnp.zeros((kv_heads, group_size, tok_rows), jnp.float32),
        jnp.zeros((kv_heads, group_size, tok_rows, head_dim), jnp.float32),
    )
    two_sided = lax.axis_size("context") == 2
    if two_sided:
        kv_pair = lax.ppermute(
            jnp.concatenate([keys_local, values_local], axis=1), "context", [(0, 1)]
        )
        keys_before, values_before = kv_pair[:, :kv_heads], kv_pair[:, kv_heads:]
        result = attend(start_state, keys_local, values_local, first_row)
        result = lax.cond(
            first_row > 0,
            lambda state: attend(state, keys_before, values_before, 0),
            lambda state: state,
            result,
        )
    else:
        keys_in = lax.all_gather(keys_local, "context", axis=0, tiled=True)
        key_rows = keys_in.shape[0]
        count_of_blocks = key_rows // tok_rows
        key_blocks = keys_in.reshape(count_of_blocks, tok_rows, kv_heads, head_dim)
        val_blocks = lax.all_gather(values_local, "context", axis=0, tiled=True).reshape(
            count_of_blocks, tok_rows, kv_heads, head_dim
        )

        def advance(current, inputs):
            key_blk, val_blk, number = inputs
            block_first = number * tok_rows

            def advance_active(state_in):
                return attend(state_in, key_blk, val_blk, block_first)

            def advance_passed(state_in):
                return state_in

            return (lax.cond(block_first <= last_query, advance_active, advance_passed, current), None)

        result, unused = lax.scan(
            advance, start_state, (key_blocks, val_blocks, jnp.arange(count_of_blocks, dtype=jnp.int32))
        )
    best, total, summed = result
    attn_exact = summed / total[..., None]
    log_total = best + jnp.log(total)
    attention_result = (
        attn_exact.astype(jnp.bfloat16).transpose(2, 0, 1, 3).reshape(tok_rows, q_heads * head_dim)
    )
    attn_out = tensor_sum(jnp.dot(attention_result, o_full, preferred_element_type=jnp.float32))
    mixed = residual_in + attn_out
    scale_two = inverse_rms(mixed)
    normed_two = (mixed * scale_two * ffn_gain).astype(jnp.bfloat16)
    hidden = jnp.dot(normed_two, gu_full, preferred_element_type=jnp.float32)
    gate, up_part = hidden[:, : w_gate.shape[1]], hidden[:, w_gate.shape[1] :]
    sigmoid_gate = jax.nn.sigmoid(gate)
    silu_gate = gate * sigmoid_gate
    activated = (silu_gate * up_part).astype(jnp.bfloat16)
    grad_top = out_grad.astype(jnp.float32)
    down_grad = jnp.einsum("tf,td->fd", activated, out_grad, preferred_element_type=jnp.float32)
    grad_act = jnp.einsum("td,fd->tf", out_grad, d_full, preferred_element_type=jnp.float32)
    silu_slope = sigmoid_gate * (1.0 + gate * (1.0 - sigmoid_gate))
    grad_gate = (grad_act * up_part * silu_slope).astype(jnp.bfloat16)
    grad_up = (grad_act * silu_gate).astype(jnp.bfloat16)
    grad_hidden = jnp.concatenate([grad_gate, grad_up], axis=1)
    hidden_grad = jnp.einsum("td,tf->df", normed_two, grad_hidden, preferred_element_type=jnp.float32)
    normed_two_part = jnp.einsum("tf,df->td", grad_hidden, gu_full, preferred_element_type=jnp.float32)
    down_share = scatter_grad(down_grad, 1)
    hidden_share = scatter_grad(hidden_grad, 0)
    ffn_gain_part = jnp.sum(normed_two_part * mixed * scale_two, axis=0)
    grad_normed_two = tensor_sum(normed_two_part)
    mlp_part = jnp.dot(activated, d_full, preferred_element_type=jnp.float32).astype(jnp.bfloat16)
    grad_mixed = grad_top + norm_backward(mixed, scale_two, ffn_gain, grad_normed_two)
    grad_mixed_low = grad_mixed.astype(jnp.bfloat16)
    out_proj_grad = jnp.einsum(
        "th,td->hd", attention_result, grad_mixed_low, preferred_element_type=jnp.float32
    )
    out_share = scatter_grad(out_proj_grad, 1)
    grad_heads = jnp.einsum(
        "td,hd->th", grad_mixed_low, o_full, preferred_element_type=jnp.float32
    ).astype(jnp.bfloat16)
    grad_rows = grad_heads.reshape(tok_rows, kv_heads, group_size, head_dim)
    grad_heads = grad_rows.transpose(1, 2, 0, 3)
    delta = jnp.sum(grad_heads.astype(jnp.float32) * attn_exact, axis=-1)
    def back_block(dq_in, key_blk, val_blk, key_first):
        allowed = block_mask(key_first, tok_rows)
        scores = (
            jnp.einsum("qkgd,skd->kgqs", grouped_q, key_blk, preferred_element_type=jnp.float32)
            * inv_sqrt
        )
        probs = jnp.where(allowed, jnp.exp(scores - log_total[..., None]), 0.0)
        grad_probs = jnp.einsum(
            "kgqd,skd->kgqs", grad_heads, val_blk, preferred_element_type=jnp.float32
        )
        grad_scores = (probs * (grad_probs - delta[..., None])).astype(jnp.bfloat16)
        dq_out = (
            dq_in
            + jnp.einsum(
                "kgqs,skd->qkgd", grad_scores, key_blk, preferred_element_type=jnp.float32
            )
            * inv_sqrt
        )
        key_part = (
            jnp.einsum(
                "kgqs,qkgd->skd", grad_scores, grouped_q, preferred_element_type=jnp.float32
            )
            * inv_sqrt
        )
        value_part = jnp.einsum(
            "kgqs,kgqd->skd",
            probs.astype(jnp.bfloat16),
            grad_heads,
            preferred_element_type=jnp.float32,
        )
        return (dq_out, key_part, value_part)

    kv_zeros = jnp.zeros((tok_rows, kv_heads, head_dim), jnp.float32)
    dq_zeros = jnp.zeros((tok_rows, kv_heads, group_size, head_dim), jnp.float32)
    if two_sided:
        dq_total, key_before, value_before = lax.cond(
            first_row > 0,
            lambda dq_in: back_block(dq_in, keys_before, values_before, 0),
            lambda dq_in: (dq_in, kv_zeros, kv_zeros),
            dq_zeros,
        )
        mlp_part, dq_total = lax.optimization_barrier((mlp_part, dq_total))
        kv_back = lax.ppermute(
            jnp.concatenate([key_before, value_before], axis=1).astype(jnp.bfloat16),
            "context",
            [(1, 0)],
        ).astype(jnp.float32)
        dq_total, grad_keys, grad_values = back_block(
            dq_total, keys_local, values_local, first_row
        )
        grad_keys = grad_keys + kv_back[:, :kv_heads]
        grad_values = grad_values + kv_back[:, kv_heads:]
    else:
        back_keys, back_values = (
            lax.all_gather(keys_local, "context", axis=0, tiled=True),
            lax.all_gather(values_local, "context", axis=0, tiled=True),
        )
        key_total = back_keys.shape[0]
        back_count = key_total // tok_rows
        key_stack = back_keys.reshape(back_count, tok_rows, kv_heads, head_dim)
        value_stack = back_values.reshape(back_count, tok_rows, kv_heads, head_dim)
        block_numbers = jnp.arange(back_count, dtype=jnp.int32)

        def backstep(dq_running, inputs):
            key_blk, val_blk, number = inputs
            key_first = number * tok_rows

            def backstep_active(dq_in):
                return back_block(dq_in, key_blk, val_blk, key_first)

            def backstep_passed(dq_in):
                return (dq_in, kv_zeros, kv_zeros)

            dq_next, key_part, value_part = lax.cond(
                key_first <= last_query, backstep_active, backstep_passed, dq_running
            )
            return (dq_next, (key_part, value_part))

        dq_total, kv_parts = lax.scan(backstep, dq_zeros, (key_stack, value_stack, block_numbers))
        key_terms = kv_parts[0].reshape(key_total, kv_heads, head_dim)
        value_terms = kv_parts[1].reshape(key_total, kv_heads, head_dim)
        grad_keys, grad_values = (
            lax.psum_scatter(
                key_terms.astype(jnp.bfloat16), "context", scatter_dimension=0, tiled=True
            ).astype(jnp.float32),
            lax.psum_scatter(
                value_terms.astype(jnp.bfloat16), "context", scatter_dimension=0, tiled=True
            ).astype(jnp.float32),
        )
    mlp_out = tensor_sum(mlp_part)
    block_out = (mixed + mlp_out).astype(jnp.bfloat16)
    grad_q_normed = rotate_back(dq_total.reshape(tok_rows, q_heads, head_dim), cosine, sine)
    q_gain_part = jnp.sum(grad_q_normed * query_raw * query_scale, axis=(0, 1))
    grad_q_raw = (
        norm_backward(query_raw, query_scale, q_gain, grad_q_normed)
        .astype(jnp.bfloat16)
        .reshape(tok_rows, q_heads * head_dim)
    )
    grad_k_normed = rotate_back(grad_keys, cosine, sine)
    k_gain_part = jnp.sum(grad_k_normed * unnormed_key * key_scale, axis=(0, 1))
    grad_k_raw = (
        norm_backward(unnormed_key, key_scale, k_gain, grad_k_normed)
        .astype(jnp.bfloat16)
        .reshape(tok_rows, kv_heads * head_dim)
    )
    grad_v_low = grad_values.astype(jnp.bfloat16).reshape(tok_rows, kv_heads * head_dim)
    grad_kv = jnp.concatenate([grad_k_raw, grad_v_low], axis=1)
    query_grad = jnp.einsum(
        "td,th->dh", first_normed, grad_q_raw, preferred_element_type=jnp.float32
    )
    kv_grad = jnp.einsum("td,th->dh", first_normed, grad_kv, preferred_element_type=jnp.float32)
    query_share = scatter_grad(query_grad, 0)
    kv_share = scatter_grad(kv_grad, 0)
    normed_one_part = jnp.einsum(
        "th,dh->td",
        jnp.concatenate([grad_q_raw, grad_kv], axis=1),
        qkv_full,
        preferred_element_type=jnp.float32,
    )
    attn_gain_part = jnp.sum(normed_one_part * residual_in * scale_one, axis=0)
    grad_normed_one = tensor_sum(normed_one_part)
    input_grad = grad_mixed + norm_backward(residual_in, scale_one, attn_gain, grad_normed_one)
    gains = sum_everywhere(
        jnp.concatenate(
            [restore(attn_gain_part), restore(ffn_gain_part), q_gain_part, k_gain_part]
        )
    )
    width = attn_gain.shape[0]
    attn_gain_grad, ffn_gain_grad = gains[:width], gains[width : 2 * width]
    q_gain_grad = gains[2 * width : 2 * width + head_dim]
    k_gain_grad = gains[2 * width + head_dim :]
    weight_grads = (
        query_share,
        kv_share[:, :k_cols],
        kv_share[:, k_cols:],
        out_share,
        hidden_share[:, : w_gate.shape[1]],
        hidden_share[:, w_gate.shape[1] :],
        down_share,
    )
    return (
        restore(block_out),
        restore(input_grad),
        attn_gain_grad,
        q_gain_grad,
        k_gain_grad,
        weight_grads[0],
        weight_grads[1],
        weight_grads[2],
        weight_grads[3],
        ffn_gain_grad,
        weight_grads[4],
        weight_grads[5],
        weight_grads[6],
    )


def solution(mesh):
    in_specs = (
        P(("fsdp", "context"), None),
        P(("fsdp", "context"), None),
        P("fsdp", None),
        P(),
        P(),
        P(),
        P("fsdp", "tensor"),
        P("fsdp", "tensor"),
        P("fsdp", "tensor"),
        P("tensor", "fsdp"),
        P(),
        P("fsdp", "tensor"),
        P("fsdp", "tensor"),
        P("tensor", "fsdp"),
    )
    out_specs = (
        P(("fsdp", "context"), None),
        P(("fsdp", "context"), None),
        P(),
        P(),
        P(),
        P("fsdp", "tensor"),
        P("fsdp", "tensor"),
        P("fsdp", "tensor"),
        P("tensor", "fsdp"),
        P(),
        P("fsdp", "tensor"),
        P("fsdp", "tensor"),
        P("tensor", "fsdp"),
    )
    return jax.shard_map(
        on_device, mesh=mesh, in_specs=in_specs, out_specs=out_specs, check_vma=False
    )
```
